32 devices in a mesh: shift: 2 (over y), node: 4 (over z), rhs: 4 (over x, core).
Axes of the slice: x: 2, y: 2, z: 4, core: 2. Of those that a mesh axis runs over, the one named last changes fastest.
Arguments:
- loads: bfloat16 [8192, 4096], P('node', ('shift', 'rhs')), parts along dimension 1, may hold values from -6 to 6
- root_loads: bfloat16 [1024, 4096], P(None, ('shift', 'rhs')), parts along dimension 1, may hold values from -6 to 6
- send_rows: int32 [8192], P('node'), may hold values from 0 to 2047, as said below
- leaf_inv: bfloat16 [16, 512, 512], P('node'), as said below
- couple: bfloat16 [16, 512, 512], P('node'), may hold values from -0.09375 to 0.09375
- couple_rows: int32 [16, 512], P('node'), may hold values from 0 to 1023, as said below
- root_inv: bfloat16 [1024, 1024], P('node'), as said below
Outputs:
- leaf_solution: bfloat16 [8192, 4096], P('node', ('shift', 'rhs')), parts along dimension 1
- root_solution: bfloat16 [1024, 4096], P(None, ('shift', 'rhs')), parts along dimension 1
The draws below stay inside these ranges and needn't reach their ends.
There are 2 independent parts, one for each index of `shift`. The reference program is written for one: setup_inputs(seed, part) draws one part's arguments, and reference() takes and returns one part's arrays. A program takes and returns all parts, laid end to end along the dimension named above; an argument that names none is the same for every part. Nothing has to cross between parts.
Inputs may be any that keep to these rules, and one draw needn't show every extreme that they name: `send_rows`: each device's 4 * 512 entries form a permutation. `couple_rows`: the 512 entries of one leaf are distinct. `leaf_inv`: each block is lower triangular with a positive diagonal. `root_inv`: lower triangular with a positive diagonal.
All inputs are finite; a program needn't handle non-finite values.
Results may differ from the reference program's by a relative error of at most 0.0061.
Values may be sent and summed in bfloat16 or wider, within the bound.
No kernel may reach another device: no remote copies, remote signals or barrier semaphores. Data moves between devices by JAX's collectives and lax.ppermute only.
A program may use at most 64 MiB of HBM per device.

```python
import jax
import jax.numpy as jnp

S = 512
R = 1024
CR = 512
LEAF_DEV = 4
NRHS = 2048
NLEAF = 16
LEAFDOF = 8192
N_NODE = 4


def lower_blocks(key, count, order):
    first, second = jax.random.split(key)
    diag_vals = jax.random.uniform(first, (count, order), jnp.float32, 0.6, 1.4)
    lower_vals = jax.random.normal(second, (count, order, order), jnp.float32) * (0.6 / order ** 0.5)
    strict = jnp.tril(jnp.ones((order, order), jnp.float32), -1)
    eye_mat = jnp.eye(order, dtype=jnp.float32)
    return lower_vals * strict[None] + diag_vals[:, :, None] * eye_mat[None]


def draw_send_rows(key, part):
    subkeys = jax.random.split(key, N_NODE)
    return jax.vmap(lambda subkey: jax.random.permutation(subkey, LEAF_DEV * S))(subkeys).reshape(-1).astype(jnp.int32)


def draw_couple_rows(key, part):
    subkeys = jax.random.split(jax.random.fold_in(key, 7), NLEAF)
    whole = jax.vmap(lambda subkey: jax.random.permutation(subkey, R))(subkeys)
    return whole[:, :CR].astype(jnp.int32)


def draw_leaf_inv(key, part):
    return lower_blocks(jax.random.fold_in(key, 11), NLEAF, S).astype(jnp.bfloat16)


def draw_root_inv(key, part):
    return lower_blocks(jax.random.fold_in(key, 13), 1, R)[0].astype(jnp.bfloat16)


def block_levels(stream_key, shape, cuts, least, largest):
    loudness, own = 1.0, jax.random.fold_in(stream_key, 6)
    for position, parts in cuts:
        heights = jnp.exp(jax.random.uniform(jax.random.fold_in(own, position), (parts,), jnp.float32, least / len(cuts), largest / len(cuts)))
        loudness = loudness * jnp.repeat(heights, shape[position] // parts).reshape([-1 if axis == position else 1 for axis in range(len(shape))])
    return loudness


def scatter_about(stream_key, shape, spread, limit, cuts=(), kind=jnp.bfloat16):
    drawn = jax.random.normal(stream_key, shape, jnp.float32) * spread
    if len(cuts) > 0:
        drawn = block_levels(stream_key, shape, cuts, -0.22, 0.18) * drawn
    return jnp.clip(drawn, min=-limit, max=limit).astype(kind)


def setup_inputs(seed: int = 0, part: int = 0) -> dict:
    streams_of = jax.random.split(jax.random.key(seed), 8)
    part_keys = jax.random.split(jax.random.fold_in(streams_of[7], part), 8)
    loads = scatter_about(part_keys[0], (LEAFDOF, NRHS), 1.0, 6.0, ((0, 4), (1, 4)))
    root_loads = scatter_about(part_keys[1], (R, NRHS), 1.0, 6.0, ((1, 4),))
    send_rows = draw_send_rows(jax.random.fold_in(streams_of[7], 71), part)
    leaf_inv = draw_leaf_inv(jax.random.fold_in(streams_of[7], 71), part)
    couple = scatter_about(streams_of[4], (NLEAF, CR, S), (S * NLEAF // 2) ** -0.5, 0.09375, ((0, 4),))
    couple_rows = draw_couple_rows(jax.random.fold_in(streams_of[7], 71), part)
    root_inv = draw_root_inv(jax.random.fold_in(streams_of[7], 71), part)
    return dict(loads=loads, root_loads=root_loads, send_rows=send_rows, leaf_inv=leaf_inv, couple=couple, couple_rows=couple_rows, root_inv=root_inv)


def reference(loads, root_loads, send_rows, leaf_inv, couple, couple_rows, root_inv):
    block_rows = LEAF_DEV * S
    slot_rows = block_rows // N_NODE
    owners = N_NODE
    source = send_rows.reshape(owners, owners, slot_rows).astype(jnp.int32)
    source = source + (jnp.arange(owners, dtype=jnp.int32) * block_rows)[:, None, None]
    source = jnp.transpose(source, (1, 0, 2)).reshape(-1)
    ordered = loads[source].reshape(NLEAF, S, NRHS)
    fwd = jnp.einsum('nij,njc->nic', leaf_inv.astype(jnp.float32), ordered.astype(jnp.float32)).astype(jnp.bfloat16)
    terms = jnp.einsum('nrj,njc->nrc', couple.astype(jnp.float32), fwd.astype(jnp.float32))
    update = jnp.zeros((R, NRHS), jnp.float32).at[couple_rows.reshape(-1)].add(terms.reshape(-1, NRHS))
    reduced = (root_loads.astype(jnp.float32) - update).astype(jnp.bfloat16)
    root_fwd = jnp.dot(root_inv, reduced, preferred_element_type=jnp.float32).astype(jnp.bfloat16)
    root_solution = jnp.dot(root_inv.T, root_fwd, preferred_element_type=jnp.float32).astype(jnp.bfloat16)
    picked = root_solution[couple_rows.reshape(-1)].reshape(NLEAF, CR, NRHS)
    backsub = jnp.einsum('nrj,nrc->njc', couple.astype(jnp.float32), picked.astype(jnp.float32))
    corrected = (fwd.astype(jnp.float32) - backsub).astype(jnp.bfloat16)
    leaf_solution = jnp.einsum('nji,njc->nic', leaf_inv.astype(jnp.float32), corrected.astype(jnp.float32)).astype(jnp.bfloat16)
    return leaf_solution.reshape(LEAFDOF, NRHS), root_solution
```

```python
import functools

import jax
import jax.numpy as jnp
from jax import lax
from jax.experimental import pallas as pl
from jax.experimental.pallas import tpu as pltpu
from jax.sharding import PartitionSpec as P

BF = jnp.bfloat16
F32 = jnp.float32
LANES = 128
VMEM_LIMIT = 24 * 1024 * 1024
NT = (((1,), (1,)), ((), ()))


def dot(a, b):
    return jnp.dot(a, b, preferred_element_type=F32)


def dot_nt(a, b):
    return lax.dot_general(a, b, NT, preferred_element_type=F32)


def any_spec():
    return pl.BlockSpec(memory_space=pl.ANY)


def vmem_spec():
    return pl.BlockSpec(memory_space=pltpu.VMEM)


def smem_spec():
    return pl.BlockSpec(memory_space=pltpu.SMEM)


def params():
    return pltpu.CompilerParams(vmem_limit_bytes=VMEM_LIMIT)


def cost(flops, moved):
    return pl.CostEstimate(flops=int(flops), bytes_accessed=int(moved), transcendentals=0)


def leader(level, group):
    if level == 0:
        return group
    return leader(level - 1, 2 * group + (1 if group % 2 == 0 else 0))


def tree(nodes):
    depth = nodes.bit_length() - 1
    ups = []
    for level in range(1, depth):
        pairs = []
        for group in range(nodes >> level):
            left, right = leader(level - 1, 2 * group), leader(level - 1, 2 * group + 1)
            pairs.append((left, right) if group % 2 == 0 else (right, left))
        ups.append(pairs)
    left, right = leader(depth - 1, 0), leader(depth - 1, 1)
    return ups, [(left, right), (right, left)]


def pick_kernel(nodes, first, count, me_ref, rows_ref, loads_ref, *rest):
    outs, held = rest[:-1], rest[-1]
    total = loads_ref.shape[0]
    block = total // nodes
    me = me_ref[0]
    tile = 128
    x = loads_ref[:, first * LANES : (first + count) * LANES]
    for k in range(total // tile):
        row = rows_ref[k : k + 1, :]
        column = jnp.broadcast_to(row, (tile, tile)).T
        parts = []
        for j in range(total // tile):
            wanted = lax.broadcasted_iota(jnp.int32, (tile, tile), 1) + j * tile
            parts.append(jnp.where(column == wanted, 1.0, 0.0).astype(BF))
        onehot = jnp.concatenate(parts, axis=1)
        held[k * tile : (k + 1) * tile, :] = dot(onehot, x).astype(BF)
    for c in range(count):
        for s in range(nodes):
            start = pl.multiple_of((me ^ s) * block, block)
            outs[c * nodes + s][...] = held[pl.ds(start, block), c * LANES : (c + 1) * LANES]


def pick(nodes, first, count, me, rows, loads):
    total = loads.shape[0]
    block = total // nodes
    width = count * LANES
    return pl.pallas_call(
        functools.partial(pick_kernel, nodes, first, count),
        in_specs=[smem_spec(), vmem_spec(), vmem_spec()],
        out_specs=[vmem_spec()] * (count * nodes),
        out_shape=[jax.ShapeDtypeStruct((block, LANES), BF)] * (count * nodes),
        scratch_shapes=[pltpu.VMEM((total, width), BF)],
        compiler_params=params(),
        cost_estimate=cost(2 * total * total * width, 4 * total * width),
        name="pick",
    )(me, rows, loads)


def identity(size):
    same = lax.broadcasted_iota(jnp.int32, (size, size), 0) == lax.broadcasted_iota(jnp.int32, (size, size), 1)
    return jnp.where(same, 1.0, 0.0).astype(BF)


def prep_kernel(rows_ref, couple_ref, inv_ref, spread_ref, spread_t_ref, inv_t_ref):
    leaves, picked, order = couple_ref.shape
    root = spread_ref.shape[0]
    eye = identity(picked)
    for n in range(leaves):
        c = couple_ref[n]
        at = slice(n * order, (n + 1) * order)
        rows = rows_ref[n : n + 1, :]
        onehot = lax.broadcasted_iota(jnp.int32, (root, picked), 0) == jnp.broadcast_to(rows, (root, picked))
        onehot = jnp.where(onehot, 1.0, 0.0).astype(BF)
        spread_ref[:, at] = dot(onehot, c).astype(BF)
        c_t = dot_nt(eye, c).astype(BF)
        spread_t_ref[at, :] = dot_nt(c_t, onehot).astype(BF)
        inv_t_ref[n] = dot_nt(identity(order), inv_ref[n]).astype(BF)


def prep(rows, couple, inv, root):
    leaves, picked, order = couple.shape
    return pl.pallas_call(
        prep_kernel,
        in_specs=[vmem_spec()] * 3,
        out_specs=[vmem_spec()] * 3,
        out_shape=[
            jax.ShapeDtypeStruct((root, leaves * order), BF),
            jax.ShapeDtypeStruct((leaves * order, root), BF),
            jax.ShapeDtypeStruct((leaves, order, order), BF),
        ],
        compiler_params=params(),
        cost_estimate=cost(2 * leaves * picked * order * (2 * root + 2 * order), leaves * order * (4 * root + 6 * order)),
        name="prep",
    )(rows, couple, inv)


def forward_kernel(nodes, me_ref, inv_ref, spread_ref, *rest):
    blocks, (fwd_ref, part_ref, wide_ref, held) = rest[:nodes], rest[nodes:]
    block = blocks[0].shape[0]
    leaves, order, _ = inv_ref.shape
    half = order // 2
    me = me_ref[0]
    for s in range(nodes):
        held[pl.ds(pl.multiple_of((me ^ s) * block, block), block), :] = blocks[s][...]
    for n in range(leaves):
        at = n * order
        x = held[at : at + order, :]
        fwd_ref[at : at + half, :] = dot(inv_ref[n, :half, :half], x[:half]).astype(BF)
        fwd_ref[at + half : at + order, :] = dot(inv_ref[n, half:, :], x).astype(BF)
    part = dot(spread_ref[...], fwd_ref[...])
    wide_ref[...] = part
    part_ref[...] = part.astype(BF)


def forward(nodes, me, inv, spread, blocks):
    leaves, order, _ = inv.shape
    root = spread.shape[0]
    return pl.pallas_call(
        functools.partial(forward_kernel, nodes),
        in_specs=[smem_spec()] + [vmem_spec()] * (2 + nodes),
        out_specs=[vmem_spec()] * 3,
        out_shape=[
            jax.ShapeDtypeStruct((leaves * order, LANES), BF),
            jax.ShapeDtypeStruct((root, LANES), BF),
            jax.ShapeDtypeStruct((root, LANES), F32),
        ],
        scratch_shapes=[pltpu.VMEM((leaves * order, LANES), BF)],
        compiler_params=params(),
        cost_estimate=cost(
            2 * leaves * order * LANES * (order + root),
            2 * leaves * order * (order + root + 3 * LANES) + 2 * root * LANES,
        ),
        name="forward",
    )(me, inv, spread, *blocks)


def root_prep_kernel(count, *rest):
    pieces, (whole_ref, whole_t_ref) = rest[:count], rest[count:]
    width = pieces[0].shape[1]
    for q in range(count):
        piece = pieces[q][...]
        whole_ref[:, q * width : (q + 1) * width] = piece
        whole_t_ref[q * width : (q + 1) * width, :] = dot_nt(identity(width), piece).astype(BF)


def root_prep(pieces):
    count = len(pieces)
    root, width = pieces[0].shape
    return pl.pallas_call(
        functools.partial(root_prep_kernel, count),
        in_specs=[vmem_spec()] * count,
        out_specs=[vmem_spec()] * 2,
        out_shape=[
            jax.ShapeDtypeStruct((root, count * width), BF),
            jax.ShapeDtypeStruct((count * width, root), BF),
        ],
        compiler_params=params(),
        cost_estimate=cost(2 * root * root * width, 6 * root * root),
        name="root_prep",
    )(*pieces)


def root_kernel(chunk, count, order_ref, whole_ref, whole_t_ref, loads_ref, one_ref, two_ref, out_ref, held, solved):
    root = whole_ref.shape[1]
    width = root // count
    update = one_ref[...].astype(F32) + two_ref[...].astype(F32)
    held[...] = (loads_ref[:, chunk * LANES : (chunk + 1) * LANES].astype(F32) - update).astype(BF)
    blocks = [held[pl.ds(pl.multiple_of(order_ref[q] * width, width), width), :] for q in range(count)]
    reduced = jnp.concatenate(blocks, axis=0)
    root_fwd = dot(whole_ref[...], reduced).astype(BF)
    solved[...] = dot(whole_t_ref[...], root_fwd).astype(BF)
    for q in range(count):
        start = pl.multiple_of(order_ref[q] * width, width)
        out_ref[pl.ds(start, width), :] = solved[q * width : (q + 1) * width, :]


def root_solve(chunk, order, whole, whole_t, root_loads, one, two):
    count = order.shape[0]
    root = whole.shape[1]
    return pl.pallas_call(
        functools.partial(root_kernel, chunk, count),
        in_specs=[smem_spec()] + [vmem_spec()] * 5,
        out_specs=vmem_spec(),
        out_shape=jax.ShapeDtypeStruct((root, LANES), BF),
        scratch_shapes=[pltpu.VMEM((root, LANES), BF), pltpu.VMEM((root, LANES), BF)],
        compiler_params=params(),
        cost_estimate=cost(4 * root * root * LANES, 4 * root * root + 8 * root * LANES),
        name="root_solve",
    )(order, whole, whole_t, root_loads, one, two)


def backward_kernel(chunk, take_ref, own_ref, got_ref, fwd_ref, spread_t_ref, inv_t_ref, *rest):
    out_ref, root_ref, held, solved, sems = rest[-5:]
    leaves, order, _ = inv_t_ref.shape
    half = order // 2
    columns = pl.ds(chunk * LANES, LANES)
    held[...] = jnp.where(take_ref[0] > 0, got_ref[...], own_ref[...])
    copies = [pltpu.make_async_copy(held, root_ref.at[:, columns], sems.at[leaves])]
    copies[0].start()
    back = dot(spread_t_ref[...], held[...])
    corrected = (fwd_ref[...].astype(F32) - back).astype(BF)
    for n in range(leaves):
        at = n * order
        x = corrected[at : at + order]
        solved[at : at + half, :] = dot(inv_t_ref[n, :half, :], x).astype(BF)
        solved[at + half : at + order, :] = dot(inv_t_ref[n, half:, half:], x[half:]).astype(BF)
        rows = pl.ds(at, order)
        copy = pltpu.make_async_copy(solved.at[rows], out_ref.at[rows, columns], sems.at[n])
        copy.start()
        copies.append(copy)
    for copy in copies:
        copy.wait()


def backward(chunk, width, take, own, got, fwd, spread_t, inv_t, before):
    leaves, order, _ = inv_t.shape
    root = spread_t.shape[1]
    inputs = [take, own, got, fwd, spread_t, inv_t]
    aliases, extra = {}, []
    if before is not None:
        aliases = {len(inputs): 0, len(inputs) + 1: 1}
        extra = list(before)
    return pl.pallas_call(
        functools.partial(backward_kernel, chunk),
        in_specs=[smem_spec()] + [vmem_spec()] * 5 + [any_spec()] * len(extra),
        out_specs=[any_spec()] * 2,
        out_shape=[
            jax.ShapeDtypeStruct((leaves * order, width), BF),
            jax.ShapeDtypeStruct((root, width), BF),
        ],
        scratch_shapes=[
            pltpu.VMEM((root, LANES), BF),
            pltpu.VMEM((leaves * order, LANES), BF),
            pltpu.SemaphoreType.DMA((leaves + 1,)),
        ],
        input_output_aliases=aliases,
        compiler_params=params(),
        cost_estimate=cost(
            2 * leaves * order * LANES * (order + root),
            2 * leaves * order * (order + root + 2 * LANES) + 6 * root * LANES,
        ),
        name="backward",
    )(*inputs, *extra)


def per_device(sizes, loads, root_loads, send_rows, leaf_inv, couple, couple_rows, root_inv):
    nodes = sizes["node"]
    root, width = root_loads.shape
    total = loads.shape[0]
    chunks = width // LANES
    ups, top = tree(nodes)
    node = lax.axis_index("node")
    me = node.astype(jnp.int32).reshape(1)
    rows = send_rows.reshape(total // 128, 128)

    stages, count = [], 1
    for axis in ("rhs", "shift"):
        if count * sizes[axis] * LANES <= root:
            bits = sizes[axis].bit_length() - 1
            stages = [(axis, bit) for bit in range(bits)] + stages if axis == "rhs" else stages + [(axis, bit) for bit in range(bits)]
            count *= sizes[axis]
    mine = jnp.int32(0)
    for place, (axis, bit) in enumerate(stages):
        mine = mine + (((lax.axis_index(axis).astype(jnp.int32) >> bit) & 1) << place)
    piece = lax.dynamic_slice_in_dim(root_inv, mine * (root // count), root // count, axis=1)
    for pairs in ups:
        piece = jnp.concatenate([piece, lax.ppermute(piece, "node", pairs)], axis=0)
    other = lax.ppermute(piece, "node", top)
    is_left = node == top[0][0]
    piece = jnp.concatenate([jnp.where(is_left, piece, other), jnp.where(is_left, other, piece)], axis=0)
    held = [(0, piece)]
    for place in reversed(range(len(stages))):
        axis, bit = stages[place]
        pairs = [(i, i ^ (1 << bit)) for i in range(sizes[axis])]
        held = held + [(q | (1 << place), lax.ppermute(x, axis, pairs)) for q, x in held]
    held.sort(key=lambda pair: pair[0])
    order = jnp.arange(count, dtype=jnp.int32) ^ mine

    sends = pick(nodes, 0, 1, me, rows, loads)
    if chunks > 1:
        sends = list(sends) + list(pick(nodes, 1, chunks - 1, me, rows, loads))
    spread, spread_t, inv_t = prep(couple_rows, couple, leaf_inv, root)
    whole, whole_t = root_prep([x for _, x in held])

    result = None
    for c in range(chunks):
        mine_blocks = sends[c * nodes : (c + 1) * nodes]
        blocks = [mine_blocks[0]]
        for s in range(1, nodes):
            blocks.append(lax.ppermute(mine_blocks[s], "node", [(i, i ^ s) for i in range(nodes)]))
        fwd, part, wide = forward(nodes, me, leaf_inv, spread, blocks)
        for pairs in ups:
            wide = wide + lax.ppermute(part, "node", pairs).astype(F32)
            part = wide.astype(BF)
        other = lax.ppermute(part, "node", top)
        own = root_solve(c, order, whole, whole_t, root_loads, part, other)
        got = own
        take = jnp.zeros((1,), jnp.int32)
        for level, pairs in enumerate(reversed(ups)):
            if level > 0:
                own = jnp.where(take[0] > 0, got, own)
            got = lax.ppermute(own, "node", [(b, a) for a, b in pairs])
            take = jnp.zeros((), jnp.int32)
            for sender, _ in pairs:
                take = take + (node == sender).astype(jnp.int32)
            take = take.reshape(1)
        result = backward(c, width, take, own, got, fwd, spread_t, inv_t, result)
    return tuple(result)


def solution(mesh):
    return jax.shard_map(
        functools.partial(per_device, dict(mesh.shape)),
        mesh=mesh,
        in_specs=(
            P("node", ("shift", "rhs")),
            P(None, ("shift", "rhs")),
            P("node"),
            P("node", None, None),
            P("node", None, None),
            P("node", None),
            P("node", None),
        ),
        out_specs=(P("node", ("shift", "rhs")), P(None, ("shift", "rhs"))),
        check_vma=False,
    )
```

```python
import functools

import jax
import jax.numpy as jnp
from jax import lax
from jax.experimental import pallas as pl
from jax.experimental.pallas import tpu as pltpu
from jax.sharding import PartitionSpec as P

BF = jnp.bfloat16
F32 = jnp.float32
LANES = 128
GROUP = 2
SHARE = 1.0
VMEM_LIMIT = 24 * 1024 * 1024
NT = (((1,), (1,)), ((), ()))


def dot(a, b):
    return jnp.dot(a, b, preferred_element_type=F32)


def dot_nt(a, b):
    return lax.dot_general(a, b, NT, preferred_element_type=F32)


def any_spec():
    return pl.BlockSpec(memory_space=pl.ANY)


def vmem_spec():
    return pl.BlockSpec(memory_space=pltpu.VMEM)


def smem_spec():
    return pl.BlockSpec(memory_space=pltpu.SMEM)


def params():
    return pltpu.CompilerParams(vmem_limit_bytes=VMEM_LIMIT)


def cost(flops, moved):
    return pl.CostEstimate(flops=int(flops * SHARE), bytes_accessed=int(moved * SHARE), transcendentals=0)


def leader(level, group):
    if level == 0:
        return group
    return leader(level - 1, 2 * group + (1 if group % 2 == 0 else 0))


def tree(nodes):
    depth = nodes.bit_length() - 1
    ups = []
    for level in range(1, depth):
        pairs = []
        for group in range(nodes >> level):
            left, right = leader(level - 1, 2 * group), leader(level - 1, 2 * group + 1)
            pairs.append((left, right) if group % 2 == 0 else (right, left))
        ups.append(pairs)
    left, right = leader(depth - 1, 0), leader(depth - 1, 1)
    return ups, [(left, right), (right, left)]


def pick_kernel(nodes, firsts, widths, me_ref, rows_ref, loads_ref, *rest):
    count = len(widths)
    outs, (picked, held, sem, sems) = rest[-count * nodes - 4 : -4], rest[-4:]
    load = pltpu.make_async_copy(loads_ref.at[:, pl.ds(firsts[0], sum(widths))], picked, sem)
    load.start()
    total = loads_ref.shape[0]
    block = total // nodes
    me = me_ref[0]
    tile = 128
    load.wait()
    x = picked[...]
    for k in range(total // tile):
        row = rows_ref[k : k + 1, :]
        column = jnp.broadcast_to(row, (tile, tile)).T
        parts = []
        for j in range(total // tile):
            wanted = lax.broadcasted_iota(jnp.int32, (tile, tile), 1) + j * tile
            parts.append(jnp.where(column == wanted, 1.0, 0.0).astype(BF))
        onehot = jnp.concatenate(parts, axis=1)
        held[k * tile : (k + 1) * tile, :] = dot(onehot, x).astype(BF)
    copies = []
    for c in range(count):
        for s in range(nodes):
            start = pl.multiple_of((me ^ s) * block, block)
            source = held.at[pl.ds(start, block), pl.ds(firsts[c] - firsts[0], widths[c])]
            copies.append(pltpu.make_async_copy(source, outs[c * nodes + s], sems.at[c * nodes + s]))
            copies[-1].start()
    for copy in copies:
        copy.wait()


def pick(nodes, firsts, widths, me, rows, loads, after):
    total = loads.shape[0]
    block = total // nodes
    width, count = sum(widths), len(widths) * nodes
    return pl.pallas_call(
        functools.partial(pick_kernel, nodes, firsts, widths),
        in_specs=[smem_spec(), vmem_spec(), any_spec()] + [any_spec()] * len(after),
        out_specs=[any_spec()] * count,
        out_shape=[jax.ShapeDtypeStruct((block, size), BF) for size in widths for _ in range(nodes)],
        scratch_shapes=[pltpu.VMEM((total, width), BF)] * 2
        + [pltpu.SemaphoreType.DMA, pltpu.SemaphoreType.DMA((count,))],
        compiler_params=params(),
        cost_estimate=cost(2 * total * total * width, 4 * total * width),
        name="pick",
    )(me, rows, loads, *after)


def identity(size):
    same = lax.broadcasted_iota(jnp.int32, (size, size), 0) == lax.broadcasted_iota(jnp.int32, (size, size), 1)
    return jnp.where(same, 1.0, 0.0).astype(BF)


def prep_kernel(rows_ref, couple_ref, inv_ref, *rest):
    outs, scratch, sems = rest[-7:-4], rest[-4:-1], rest[-1]
    spread_ref, spread_t_ref, inv_t_ref = scratch
    leaves, picked, order = couple_ref.shape
    root = spread_ref.shape[0]
    copies = []
    for n in range(leaves):
        c = couple_ref[n]
        at = slice(n * order, (n + 1) * order)
        rows = rows_ref[n : n + 1, :]
        onehot = lax.broadcasted_iota(jnp.int32, (root, picked), 0) == jnp.broadcast_to(rows, (root, picked))
        onehot = jnp.where(onehot, 1.0, 0.0).astype(BF)
        spread_ref[:, at] = dot(onehot, c).astype(BF)
        spread_t_ref[at, :] = dot_nt(c.T, onehot).astype(BF)
        inv_t_ref[n] = inv_ref[n].T
        places = [(slice(None), pl.ds(n * order, order)), (pl.ds(n * order, order),), (n,)]
        for k, place in enumerate(places):
            copies.append(pltpu.make_async_copy(scratch[k].at[place], outs[k].at[place], sems.at[k, n]))
            copies[-1].start()
    for copy in copies:
        copy.wait()


def prep(rows, couple, inv, root, after):
    leaves, picked, order = couple.shape
    shapes = [(root, leaves * order), (leaves * order, root), (leaves, order, order)]
    return pl.pallas_call(
        prep_kernel,
        in_specs=[vmem_spec()] * 3 + [any_spec()] * len(after),
        out_specs=[any_spec()] * 3,
        out_shape=[jax.ShapeDtypeStruct(shape, BF) for shape in shapes],
        scratch_shapes=[pltpu.VMEM(shape, BF) for shape in shapes] + [pltpu.SemaphoreType.DMA((3, leaves))],
        compiler_params=params(),
        cost_estimate=cost(2 * leaves * picked * order * (2 * root + 2 * order), leaves * order * (4 * root + 6 * order)),
        name="prep",
    )(rows, couple, inv, *after)


def forward_kernel(nodes, chunks, me_ref, inv_ref, spread_ref, *rest):
    blocks, (out_ref, *outs), (held, fwd_ref, sem) = rest[:nodes], rest[nodes:-3], rest[-3:]
    block = blocks[0].shape[0]
    leaves, order, _ = inv_ref.shape
    half = order // 2
    me = me_ref[0]
    for s in range(nodes):
        held[pl.ds(pl.multiple_of((me ^ s) * block, block), block), :] = blocks[s][...]
    for n in range(leaves):
        at = n * order
        x = held[at : at + order, :]
        fwd_ref[at : at + half, :] = dot(inv_ref[n, :half, :half], x[:half]).astype(BF)
        fwd_ref[at + half : at + order, :] = dot(inv_ref[n, half:, :], x).astype(BF)
    copy = pltpu.make_async_copy(fwd_ref, out_ref, sem)
    copy.start()
    root = spread_ref.shape[0]
    tile = min(256, root)
    for t in range(root // tile):
        at = slice(t * tile, (t + 1) * tile)
        part = dot(spread_ref[at, :], fwd_ref[...])
        for c in range(chunks):
            piece = part[:, c * LANES : (c + 1) * LANES]
            outs[c][at, :] = piece.astype(BF)
            outs[chunks + c][at, :] = piece
    copy.wait()


def forward(nodes, me, inv, spread, blocks):
    leaves, order, _ = inv.shape
    root = spread.shape[0]
    width = blocks[0].shape[1]
    chunks = width // LANES
    return pl.pallas_call(
        functools.partial(forward_kernel, nodes, chunks),
        in_specs=[smem_spec()] + [vmem_spec()] * (2 + nodes),
        out_specs=[any_spec()] + [vmem_spec()] * (2 * chunks),
        out_shape=[jax.ShapeDtypeStruct((leaves * order, width), BF)]
        + [jax.ShapeDtypeStruct((root, LANES), BF)] * chunks
        + [jax.ShapeDtypeStruct((root, LANES), F32)] * chunks,
        scratch_shapes=[pltpu.VMEM((leaves * order, width), BF)] * 2 + [pltpu.SemaphoreType.DMA],
        compiler_params=params(),
        cost_estimate=cost(
            2 * leaves * order * width * (order + root),
            2 * leaves * order * (order + root + 3 * width) + 6 * root * width,
        ),
        name="forward",
    )(me, inv, spread, *blocks)


def piece_kernel(width, mine_ref, inv_ref, *rest):
    out_ref, sem = rest[-2:]
    start = pl.multiple_of(mine_ref[0] * width, width)
    copy = pltpu.make_async_copy(inv_ref.at[:, pl.ds(start, width)], out_ref, sem)
    copy.start()
    copy.wait()


def take_piece(mine, root_inv, count, after):
    rows, root = root_inv.shape
    width = root // count
    return pl.pallas_call(
        functools.partial(piece_kernel, width),
        in_specs=[smem_spec()] + [any_spec()] * (1 + len(after)),
        out_specs=any_spec(),
        out_shape=jax.ShapeDtypeStruct((rows, width), BF),
        scratch_shapes=[pltpu.SemaphoreType.DMA],
        compiler_params=params(),
        cost_estimate=cost(0, 4 * rows * width),
        name="piece",
    )(mine, root_inv, *after)


def gather_kernel(nodes, me_ref, *rest):
    pieces, (out_ref, sems) = rest[:nodes], rest[-2:]
    rows = pieces[0].shape[0]
    copies = []
    for s in range(nodes):
        at = pl.ds(pl.multiple_of((me_ref[0] ^ s) * rows, rows), rows)
        copies.append(pltpu.make_async_copy(pieces[s], out_ref.at[at], sems.at[s]))
        copies[-1].start()
    for copy in copies:
        copy.wait()


def gather_rows(nodes, me, pieces, after):
    rows, width = pieces[0].shape
    return pl.pallas_call(
        functools.partial(gather_kernel, nodes),
        in_specs=[smem_spec()] + [any_spec()] * (nodes + len(after)),
        out_specs=any_spec(),
        out_shape=jax.ShapeDtypeStruct((nodes * rows, width), BF),
        scratch_shapes=[pltpu.SemaphoreType.DMA((nodes,))],
        compiler_params=params(),
        cost_estimate=cost(0, 4 * nodes * rows * width),
        name="gather_rows",
    )(me, *pieces, *after)


def root_prep_kernel(places, count, mine_ref, pieces_ref, *rest):
    whole_ref, whole_t_ref = rest[-2:]
    root = whole_ref.shape[0]
    width, rows = root // count, root // len(places)
    for q in range(count):
        at = pl.ds(pl.multiple_of((mine_ref[0] ^ q) * width, width), width)
        for k, place in enumerate(places):
            start = q * root + k * rows
            whole_ref[place * rows : (place + 1) * rows, at] = pieces_ref[start : start + rows, :]
    for t in range(count):
        whole_t_ref[t * width : (t + 1) * width, :] = whole_ref[:, t * width : (t + 1) * width].T


def root_prep(mine, places, count, pieces, after):
    root = pieces.shape[1] * count
    return pl.pallas_call(
        functools.partial(root_prep_kernel, places, count),
        in_specs=[smem_spec(), vmem_spec()] + [any_spec()] * len(after),
        out_specs=[vmem_spec()] * 2,
        out_shape=[jax.ShapeDtypeStruct((root, root), BF)] * 2,
        compiler_params=params(),
        cost_estimate=cost(root * root, 6 * root * root),
        name="root_prep",
    )(mine, pieces, *after)


def root_kernel(first, whole_ref, whole_t_ref, loads_ref, one_ref, two_ref, *rest):
    out_ref, reduced, solved = rest[-3:]
    root = whole_ref.shape[0]
    tile = min(256, root)
    update = one_ref[...].astype(F32) + two_ref[...].astype(F32)
    reduced[...] = (loads_ref[:, first : first + out_ref.shape[1]].astype(F32) - update).astype(BF)
    for t in range(root // tile):
        at = slice(t * tile, (t + 1) * tile)
        solved[at, :] = dot(whole_ref[at, : (t + 1) * tile], reduced[: (t + 1) * tile, :]).astype(BF)
    for t in range(root // tile):
        at = slice(t * tile, (t + 1) * tile)
        out_ref[at, :] = dot(whole_t_ref[at, t * tile :], solved[t * tile :, :]).astype(BF)


def root_solve(first, whole, whole_t, root_loads, one, two, after):
    root, width = one.shape
    return pl.pallas_call(
        functools.partial(root_kernel, first),
        in_specs=[vmem_spec()] * 5 + [any_spec()] * len(after),
        out_specs=vmem_spec(),
        out_shape=jax.ShapeDtypeStruct((root, width), BF),
        scratch_shapes=[pltpu.VMEM((root, width), BF)] * 2,
        compiler_params=params(),
        cost_estimate=cost(4 * root * root * width, 4 * root * root + 8 * root * width),
        name="root_solve",
    )(whole, whole_t, root_loads, one, two, *after)


def backward_kernel(first, count, take_ref, fwd_ref, spread_t_ref, inv_t_ref, *rest):
    owns, gots = rest[:count], rest[count : 2 * count]
    out_ref, root_ref, held, solved, sems = rest[-5:]
    leaves, order, _ = inv_t_ref.shape
    half = order // 2
    columns = pl.ds(first, held.shape[1])
    for c in range(count):
        held[:, c * LANES : (c + 1) * LANES] = jnp.where(take_ref[0] > 0, gots[c][...], owns[c][...])
    copies = [pltpu.make_async_copy(held, root_ref.at[:, columns], sems.at[leaves])]
    copies[0].start()
    root_solution = held[...]
    for n in range(leaves):
        at = n * order
        back = dot(spread_t_ref[at : at + order, :], root_solution)
        x = (fwd_ref[at : at + order, first : first + held.shape[1]].astype(F32) - back).astype(BF)
        solved[at : at + half, :] = dot(inv_t_ref[n, :half, :], x).astype(BF)
        solved[at + half : at + order, :] = dot(inv_t_ref[n, half:, half:], x[half:]).astype(BF)
        rows = pl.ds(at, order)
        copy = pltpu.make_async_copy(solved.at[rows], out_ref.at[rows, columns], sems.at[n])
        copy.start()
        copies.append(copy)
    for copy in copies:
        copy.wait()


def backward(first, total, take, owns, gots, fwd, spread_t, inv_t, before):
    leaves, order, _ = inv_t.shape
    count = len(owns)
    root, width = spread_t.shape[1], count * LANES
    inputs = [take, fwd, spread_t, inv_t, *owns, *gots]
    aliases, extra = {}, []
    if before is not None:
        aliases = {len(inputs): 0, len(inputs) + 1: 1}
        extra = list(before)
    return pl.pallas_call(
        functools.partial(backward_kernel, first, count),
        in_specs=[smem_spec()] + [vmem_spec()] * (len(inputs) - 1) + [any_spec()] * len(extra),
        out_specs=[any_spec()] * 2,
        out_shape=[
            jax.ShapeDtypeStruct((leaves * order, total), BF),
            jax.ShapeDtypeStruct((root, total), BF),
        ],
        scratch_shapes=[
            pltpu.VMEM((root, width), BF),
            pltpu.VMEM((leaves * order, width), BF),
            pltpu.SemaphoreType.DMA((leaves + 1,)),
        ],
        input_output_aliases=aliases,
        compiler_params=params(),
        cost_estimate=cost(
            2 * leaves * order * width * (order + root),
            2 * leaves * order * (order + root + 2 * width) + 6 * root * width,
        ),
        name="backward",
    )(*inputs, *extra)


def per_device(sizes, loads, root_loads, send_rows, leaf_inv, couple, couple_rows, root_inv):
    nodes = sizes["node"]
    root, width = root_loads.shape
    total = loads.shape[0]
    chunks = width // LANES
    ups, top = tree(nodes)
    node = lax.axis_index("node")
    me = node.astype(jnp.int32).reshape(1)
    rows = send_rows.reshape(total // 128, 128)

    stages, count = [], 1
    for axis in ("rhs", "shift"):
        if count * sizes[axis] * LANES <= root:
            bits = sizes[axis].bit_length() - 1
            stages = [(axis, bit) for bit in reversed(range(bits))] + stages
            count *= sizes[axis]
    mine = jnp.int32(0)
    for place, (axis, bit) in enumerate(stages):
        mine = mine + (((lax.axis_index(axis).astype(jnp.int32) >> bit) & 1) << place)
    mine = mine.reshape(1)
    places = list(range(nodes))

    piece = take_piece(mine, root_inv, count, [])
    pieces = [piece]
    for s in range(1, nodes):
        pieces.append(lax.ppermute(piece, "node", [(i, i ^ s) for i in range(nodes) if i ^ s in top[0]]))
    sent = pick(nodes, [0], [width], me, rows, loads, [])
    piece = gather_rows(nodes, me, pieces, [sent[0]])
    for axis, bit in stages:
        pairs = [(i, i ^ (1 << bit)) for i in range(sizes[axis])]
        piece = jnp.concatenate([piece, lax.ppermute(piece, axis, pairs)], axis=0)

    blocks = [sent[0]] + [lax.ppermute(sent[s], "node", [(i, i ^ s) for i in range(nodes)]) for s in range(1, nodes)]
    spread, spread_t, inv_t = prep(couple_rows, couple, leaf_inv, root, [sent[0]])
    whole, whole_t = root_prep(mine, places, count, piece, [])
    fwd, *parts = forward(nodes, me, leaf_inv, spread, blocks)
    result, owns, gots = None, [], []
    for c in range(chunks):
        part, wide = parts[c], parts[chunks + c]
        for pairs in ups:
            wide = wide + lax.ppermute(part, "node", pairs).astype(F32)
            part = wide.astype(BF)
        other = lax.ppermute(part, "node", top)
        own = root_solve(c * LANES, whole, whole_t, root_loads, part, other, [])
        got, take = own, jnp.zeros((1,), jnp.int32)
        for level, pairs in enumerate(reversed(ups)):
            if level > 0:
                own = jnp.where(take[0] > 0, got, own)
            got = lax.ppermute(own, "node", [(b, a) for a, b in pairs])
            take = jnp.zeros((1,), jnp.int32)
            for sender, _ in pairs:
                take = take + (node == sender).astype(jnp.int32)
        owns.append(own)
        gots.append(got)
        if len(owns) == GROUP or c == chunks - 1:
            first = (c + 1 - len(owns)) * LANES
            result = backward(first, width, take, owns, gots, fwd, spread_t, inv_t, result)
            owns, gots = [], []
    return tuple(result)


def solution(mesh):
    return jax.shard_map(
        functools.partial(per_device, dict(mesh.shape)),
        mesh=mesh,
        in_specs=(
            P("node", ("shift", "rhs")),
            P(None, ("shift", "rhs")),
            P("node"),
            P("node", None, None),
            P("node", None, None),
            P("node", None),
            P("node", None),
        ),
        out_specs=(P("node", ("shift", "rhs")), P(None, ("shift", "rhs"))),
        check_vma=False,
    )
```

```python
import functools

import jax
import jax.numpy as jnp
from jax import lax
from jax.experimental import pallas as pl
from jax.experimental.pallas import tpu as pltpu
from jax.sharding import PartitionSpec as P

BF = jnp.bfloat16
F32 = jnp.float32
LANES = 128
GROUP = 2
SHARE = 1.0
VMEM_LIMIT = 24 * 1024 * 1024
NT = (((1,), (1,)), ((), ()))


def dot(a, b):
    return jnp.dot(a, b, preferred_element_type=F32)


def dot_nt(a, b):
    return lax.dot_general(a, b, NT, preferred_element_type=F32)


def any_spec():
    return pl.BlockSpec(memory_space=pl.ANY)


def vmem_spec():
    return pl.BlockSpec(memory_space=pltpu.VMEM)


def smem_spec():
    return pl.BlockSpec(memory_space=pltpu.SMEM)


def params():
    return pltpu.CompilerParams(vmem_limit_bytes=VMEM_LIMIT)


def cost(flops, moved):
    return pl.CostEstimate(flops=int(flops * SHARE), bytes_accessed=int(moved * SHARE), transcendentals=0)


def leader(level, group):
    if level == 0:
        return group
    return leader(level - 1, 2 * group + (1 if group % 2 == 0 else 0))


def tree(nodes):
    depth = nodes.bit_length() - 1
    ups = []
    for level in range(1, depth):
        pairs = []
        for group in range(nodes >> level):
            left, right = leader(level - 1, 2 * group), leader(level - 1, 2 * group + 1)
            pairs.append((left, right) if group % 2 == 0 else (right, left))
        ups.append(pairs)
    left, right = leader(depth - 1, 0), leader(depth - 1, 1)
    return ups, [(left, right), (right, left)]


def pick_kernel(nodes, firsts, widths, me_ref, rows_ref, loads_ref, *rest):
    count = len(widths)
    outs, (picked, held, sem, sems) = rest[-count * nodes - 4 : -4], rest[-4:]
    load = pltpu.make_async_copy(loads_ref.at[:, pl.ds(firsts[0], sum(widths))], picked, sem)
    load.start()
    total = loads_ref.shape[0]
    block = total // nodes
    me = me_ref[0]
    tile = 128
    load.wait()
    x = picked[...]
    for k in range(total // tile):
        row = rows_ref[k : k + 1, :]
        column = jnp.broadcast_to(row, (tile, tile)).T
        parts = []
        for j in range(total // tile):
            wanted = lax.broadcasted_iota(jnp.int32, (tile, tile), 1) + j * tile
            parts.append(jnp.where(column == wanted, 1.0, 0.0).astype(BF))
        onehot = jnp.concatenate(parts, axis=1)
        held[k * tile : (k + 1) * tile, :] = dot(onehot, x).astype(BF)
    copies = []
    for c in range(count):
        for s in range(nodes):
            start = pl.multiple_of((me ^ s) * block, block)
            source = held.at[pl.ds(start, block), pl.ds(firsts[c] - firsts[0], widths[c])]
            copies.append(pltpu.make_async_copy(source, outs[c * nodes + s], sems.at[c * nodes + s]))
            copies[-1].start()
    for copy in copies:
        copy.wait()


def pick(nodes, firsts, widths, me, rows, loads, after):
    total = loads.shape[0]
    block = total // nodes
    width, count = sum(widths), len(widths) * nodes
    return pl.pallas_call(
        functools.partial(pick_kernel, nodes, firsts, widths),
        in_specs=[smem_spec(), vmem_spec(), any_spec()] + [any_spec()] * len(after),
        out_specs=[any_spec()] * count,
        out_shape=[jax.ShapeDtypeStruct((block, size), BF) for size in widths for _ in range(nodes)],
        scratch_shapes=[pltpu.VMEM((total, width), BF)] * 2
        + [pltpu.SemaphoreType.DMA, pltpu.SemaphoreType.DMA((count,))],
        compiler_params=params(),
        cost_estimate=cost(2 * total * total * width, 4 * total * width),
        name="pick",
    )(me, rows, loads, *after)


def identity(size):
    same = lax.broadcasted_iota(jnp.int32, (size, size), 0) == lax.broadcasted_iota(jnp.int32, (size, size), 1)
    return jnp.where(same, 1.0, 0.0).astype(BF)


def prep_kernel(rows_ref, couple_ref, inv_ref, *rest):
    outs, scratch, sems = rest[-7:-4], rest[-4:-1], rest[-1]
    spread_ref, spread_t_ref, inv_t_ref = scratch
    leaves, picked, order = couple_ref.shape
    root = spread_ref.shape[0]
    copies = []
    for n in range(leaves):
        c = couple_ref[n]
        at = slice(n * order, (n + 1) * order)
        rows = rows_ref[n : n + 1, :]
        onehot = lax.broadcasted_iota(jnp.int32, (root, picked), 0) == jnp.broadcast_to(rows, (root, picked))
        onehot = jnp.where(onehot, 1.0, 0.0).astype(BF)
        spread_ref[:, at] = dot(onehot, c).astype(BF)
        spread_t_ref[at, :] = dot_nt(c.T, onehot).astype(BF)
        inv_t_ref[n] = inv_ref[n].T
        places = [(slice(None), pl.ds(n * order, order)), (pl.ds(n * order, order),), (n,)]
        for k, place in enumerate(places):
            copies.append(pltpu.make_async_copy(scratch[k].at[place], outs[k].at[place], sems.at[k, n]))
            copies[-1].start()
    for copy in copies:
        copy.wait()


def prep(rows, couple, inv, root, after):
    leaves, picked, order = couple.shape
    shapes = [(root, leaves * order), (leaves * order, root), (leaves, order, order)]
    return pl.pallas_call(
        prep_kernel,
        in_specs=[vmem_spec()] * 3 + [any_spec()] * len(after),
        out_specs=[any_spec()] * 3,
        out_shape=[jax.ShapeDtypeStruct(shape, BF) for shape in shapes],
        scratch_shapes=[pltpu.VMEM(shape, BF) for shape in shapes] + [pltpu.SemaphoreType.DMA((3, leaves))],
        compiler_params=params(),
        cost_estimate=cost(2 * leaves * picked * order * (2 * root + 2 * order), leaves * order * (4 * root + 6 * order)),
        name="prep",
    )(rows, couple, inv, *after)


def forward_kernel(nodes, chunks, me_ref, inv_ref, spread_ref, *rest):
    blocks, (out_ref, *outs), (held, fwd_ref, sem) = rest[:nodes], rest[nodes:-3], rest[-3:]
    block = blocks[0].shape[0]
    leaves, order, _ = inv_ref.shape
    half = order // 2
    me = me_ref[0]
    for s in range(nodes):
        held[pl.ds(pl.multiple_of((me ^ s) * block, block), block), :] = blocks[s][...]
    for n in range(leaves):
        at = n * order
        x = held[at : at + order, :]
        fwd_ref[at : at + half, :] = dot(inv_ref[n, :half, :half], x[:half]).astype(BF)
        fwd_ref[at + half : at + order, :] = dot(inv_ref[n, half:, :], x).astype(BF)
    copy = pltpu.make_async_copy(fwd_ref, out_ref, sem)
    copy.start()
    root = spread_ref.shape[0]
    tile = min(256, root)
    for t in range(root // tile):
        at = slice(t * tile, (t + 1) * tile)
        part = dot(spread_ref[at, :], fwd_ref[...])
        for c in range(chunks):
            piece = part[:, c * LANES : (c + 1) * LANES]
            outs[c][at, :] = piece.astype(BF)
            outs[chunks + c][at, :] = piece
    copy.wait()


def forward(nodes, me, inv, spread, blocks):
    leaves, order, _ = inv.shape
    root = spread.shape[0]
    width = blocks[0].shape[1]
    chunks = width // LANES
    return pl.pallas_call(
        functools.partial(forward_kernel, nodes, chunks),
        in_specs=[smem_spec()] + [vmem_spec()] * (2 + nodes),
        out_specs=[any_spec()] + [vmem_spec()] * (2 * chunks),
        out_shape=[jax.ShapeDtypeStruct((leaves * order, width), BF)]
        + [jax.ShapeDtypeStruct((root, LANES), BF)] * chunks
        + [jax.ShapeDtypeStruct((root, LANES), F32)] * chunks,
        scratch_shapes=[pltpu.VMEM((leaves * order, width), BF)] * 2 + [pltpu.SemaphoreType.DMA],
        compiler_params=params(),
        cost_estimate=cost(
            40 * leaves * order * width * (order + root),
            40 * leaves * order * (order + root + 3 * width) + 6 * root * width,
        ),
        name="forward",
    )(me, inv, spread, *blocks)


def piece_kernel(width, mine_ref, inv_ref, *rest):
    out_ref, sem = rest[-2:]
    start = pl.multiple_of(mine_ref[0] * width, width)
    copy = pltpu.make_async_copy(inv_ref.at[:, pl.ds(start, width)], out_ref, sem)
    copy.start()
    copy.wait()


def take_piece(mine, root_inv, count, after):
    rows, root = root_inv.shape
    width = root // count
    return pl.pallas_call(
        functools.partial(piece_kernel, width),
        in_specs=[smem_spec()] + [any_spec()] * (1 + len(after)),
        out_specs=any_spec(),
        out_shape=jax.ShapeDtypeStruct((rows, width), BF),
        scratch_shapes=[pltpu.SemaphoreType.DMA],
        compiler_params=params(),
        cost_estimate=cost(0, 4 * rows * width),
        name="piece",
    )(mine, root_inv, *after)


def gather_kernel(nodes, me_ref, *rest):
    pieces, (out_ref, sems) = rest[:nodes], rest[-2:]
    rows = pieces[0].shape[0]
    copies = []
    for s in range(nodes):
        at = pl.ds(pl.multiple_of((me_ref[0] ^ s) * rows, rows), rows)
        copies.append(pltpu.make_async_copy(pieces[s], out_ref.at[at], sems.at[s]))
        copies[-1].start()
    for copy in copies:
        copy.wait()


def gather_rows(nodes, me, pieces, after):
    rows, width = pieces[0].shape
    return pl.pallas_call(
        functools.partial(gather_kernel, nodes),
        in_specs=[smem_spec()] + [any_spec()] * (nodes + len(after)),
        out_specs=any_spec(),
        out_shape=jax.ShapeDtypeStruct((nodes * rows, width), BF),
        scratch_shapes=[pltpu.SemaphoreType.DMA((nodes,))],
        compiler_params=params(),
        cost_estimate=cost(0, 4 * nodes * rows * width),
        name="gather_rows",
    )(me, *pieces, *after)


def root_prep_kernel(places, count, mine_ref, pieces_ref, *rest):
    whole_ref, whole_t_ref = rest[-2:]
    root = whole_ref.shape[0]
    width, rows = root // count, root // len(places)
    for q in range(count):
        at = pl.ds(pl.multiple_of((mine_ref[0] ^ q) * width, width), width)
        for k, place in enumerate(places):
            start = q * root + k * rows
            whole_ref[place * rows : (place + 1) * rows, at] = pieces_ref[start : start + rows, :]
    for t in range(count):
        whole_t_ref[t * width : (t + 1) * width, :] = whole_ref[:, t * width : (t + 1) * width].T


def root_prep(mine, places, count, pieces, after):
    root = pieces.shape[1] * count
    return pl.pallas_call(
        functools.partial(root_prep_kernel, places, count),
        in_specs=[smem_spec(), vmem_spec()] + [any_spec()] * len(after),
        out_specs=[vmem_spec()] * 2,
        out_shape=[jax.ShapeDtypeStruct((root, root), BF)] * 2,
        compiler_params=params(),
        cost_estimate=cost(root * root, 6 * root * root),
        name="root_prep",
    )(mine, pieces, *after)


def root_kernel(first, whole_ref, whole_t_ref, loads_ref, one_ref, two_ref, *rest):
    out_ref, reduced, solved = rest[-3:]
    root = whole_ref.shape[0]
    tile = min(256, root)
    update = one_ref[...].astype(F32) + two_ref[...].astype(F32)
    reduced[...] = (loads_ref[:, first : first + out_ref.shape[1]].astype(F32) - update).astype(BF)
    for t in range(root // tile):
        at = slice(t * tile, (t + 1) * tile)
        solved[at, :] = dot(whole_ref[at, : (t + 1) * tile], reduced[: (t + 1) * tile, :]).astype(BF)
    for t in range(root // tile):
        at = slice(t * tile, (t + 1) * tile)
        out_ref[at, :] = dot(whole_t_ref[at, t * tile :], solved[t * tile :, :]).astype(BF)


def root_solve(first, whole, whole_t, root_loads, one, two, after):
    root, width = one.shape
    return pl.pallas_call(
        functools.partial(root_kernel, first),
        in_specs=[vmem_spec()] * 5 + [any_spec()] * len(after),
        out_specs=vmem_spec(),
        out_shape=jax.ShapeDtypeStruct((root, width), BF),
        scratch_shapes=[pltpu.VMEM((root, width), BF)] * 2,
        compiler_params=params(),
        cost_estimate=cost(4 * root * root * width, 4 * root * root + 8 * root * width),
        name="root_solve",
    )(whole, whole_t, root_loads, one, two, *after)


def backward_kernel(first, count, take_ref, fwd_ref, spread_t_ref, inv_t_ref, *rest):
    owns, gots = rest[:count], rest[count : 2 * count]
    out_ref, root_ref, held, solved, sems = rest[-5:]
    leaves, order, _ = inv_t_ref.shape
    half = order // 2
    columns = pl.ds(first, held.shape[1])
    for c in range(count):
        held[:, c * LANES : (c + 1) * LANES] = jnp.where(take_ref[0] > 0, gots[c][...], owns[c][...])
    copies = [pltpu.make_async_copy(held, root_ref.at[:, columns], sems.at[leaves])]
    copies[0].start()
    root_solution = held[...]
    for n in range(leaves):
        at = n * order
        back = dot(spread_t_ref[at : at + order, :], root_solution)
        x = (fwd_ref[at : at + order, :].astype(F32) - back).astype(BF)
        solved[at : at + half, :] = dot(inv_t_ref[n, :half, :], x).astype(BF)
        solved[at + half : at + order, :] = dot(inv_t_ref[n, half:, half:], x[half:]).astype(BF)
        rows = pl.ds(at, order)
        copy = pltpu.make_async_copy(solved.at[rows], out_ref.at[rows, columns], sems.at[n])
        copy.start()
        copies.append(copy)
    for copy in copies:
        copy.wait()


def backward(first, total, take, owns, gots, fwd, spread_t, inv_t, before):
    leaves, order, _ = inv_t.shape
    count = len(owns)
    root, width = spread_t.shape[1], count * LANES
    inputs = [take, fwd, spread_t, inv_t, *owns, *gots]
    aliases, extra = {}, []
    if before is not None:
        aliases = {len(inputs): 0, len(inputs) + 1: 1}
        extra = list(before)
    return pl.pallas_call(
        functools.partial(backward_kernel, first, count),
        in_specs=[smem_spec()] + [vmem_spec()] * (len(inputs) - 1) + [any_spec()] * len(extra),
        out_specs=[any_spec()] * 2,
        out_shape=[
            jax.ShapeDtypeStruct((leaves * order, total), BF),
            jax.ShapeDtypeStruct((root, total), BF),
        ],
        scratch_shapes=[
            pltpu.VMEM((root, width), BF),
            pltpu.VMEM((leaves * order, width), BF),
            pltpu.SemaphoreType.DMA((leaves + 1,)),
        ],
        input_output_aliases=aliases,
        compiler_params=params(),
        cost_estimate=cost(
            2 * leaves * order * width * (order + root),
            2 * leaves * order * (order + root + 2 * width) + 6 * root * width,
        ),
        name="backward",
    )(*inputs, *extra)


def per_device(sizes, loads, root_loads, send_rows, leaf_inv, couple, couple_rows, root_inv):
    nodes = sizes["node"]
    root, width = root_loads.shape
    total = loads.shape[0]
    ups, top = tree(nodes)
    node = lax.axis_index("node")
    me = node.astype(jnp.int32).reshape(1)
    rows = send_rows.reshape(total // 128, 128)

    stages, count = [], 1
    for axis in ("rhs", "shift"):
        if count * sizes[axis] * LANES <= root:
            bits = sizes[axis].bit_length() - 1
            stages = [(axis, bit) for bit in reversed(range(bits))] + stages
            count *= sizes[axis]
    mine = jnp.int32(0)
    for place, (axis, bit) in enumerate(stages):
        mine = mine + (((lax.axis_index(axis).astype(jnp.int32) >> bit) & 1) << place)
    mine = mine.reshape(1)
    places = list(range(nodes))

    sizes_of = [min(GROUP * LANES, width - first) for first in range(0, width, GROUP * LANES)]
    firsts = [sum(sizes_of[:g]) for g in range(len(sizes_of))]
    sent = pick(nodes, firsts, sizes_of, me, rows, loads, [])
    piece = take_piece(mine, root_inv, count, [sent[0]])
    pieces = [piece]
    for s in range(1, nodes):
        pieces.append(lax.ppermute(piece, "node", [(i, i ^ s) for i in range(nodes) if i ^ s in top[0]]))
    piece = gather_rows(nodes, me, pieces, [sent[0]])
    for axis, bit in stages:
        pairs = [(i, i ^ (1 << bit)) for i in range(sizes[axis])]
        piece = jnp.concatenate([piece, lax.ppermute(piece, axis, pairs)], axis=0)

    blocks = []
    for g in range(len(sizes_of)):
        own = sent[g * nodes : (g + 1) * nodes]
        pairs = [[(i, i ^ s) for i in range(nodes)] for s in range(nodes)]
        blocks.append([own[0]] + [lax.ppermute(own[s], "node", pairs[s]) for s in range(1, nodes)])
    spread, spread_t, inv_t = prep(couple_rows, couple, leaf_inv, root, [sent[0]])
    whole, whole_t = root_prep(mine, places, count, piece, [])
    result = None
    for g in range(len(sizes_of)):
        fwd, *parts = forward(nodes, me, leaf_inv, spread, blocks[g])
        owns, gots = [], []
        chunks = sizes_of[g] // LANES
        for c in range(chunks):
            part, wide = parts[c], parts[chunks + c]
            for pairs in ups:
                wide = wide + lax.ppermute(part, "node", pairs).astype(F32)
                part = wide.astype(BF)
            other = lax.ppermute(part, "node", top)
            own = root_solve(firsts[g] + c * LANES, whole, whole_t, root_loads, part, other, [])
            got, take = own, jnp.zeros((1,), jnp.int32)
            for level, pairs in enumerate(reversed(ups)):
                if level > 0:
                    own = jnp.where(take[0] > 0, got, own)
                got = lax.ppermute(own, "node", [(b, a) for a, b in pairs])
                take = jnp.zeros((1,), jnp.int32)
                for sender, _ in pairs:
                    take = take + (node == sender).astype(jnp.int32)
            owns.append(own)
            gots.append(got)
        result = backward(firsts[g], width, take, owns, gots, fwd, spread_t, inv_t, result)
    return tuple(result)


def solution(mesh):
    return jax.shard_map(
        functools.partial(per_device, dict(mesh.shape)),
        mesh=mesh,
        in_specs=(
            P("node", ("shift", "rhs")),
            P(None, ("shift", "rhs")),
            P("node"),
            P("node", None, None),
            P("node", None, None),
            P("node", None),
            P("node", None),
        ),
        out_specs=(P("node", ("shift", "rhs")), P(None, ("shift", "rhs"))),
        check_vma=False,
    )
```

```python
import functools

import jax
import jax.numpy as jnp
from jax import lax
from jax.experimental import pallas as pl
from jax.experimental.pallas import tpu as pltpu
from jax.sharding import PartitionSpec as P

BF = jnp.bfloat16
F32 = jnp.float32
LANES = 128
GROUP = 2
SHARE = 1.0
VMEM_LIMIT = 24 * 1024 * 1024
NT = (((1,), (1,)), ((), ()))


def dot(a, b):
    return jnp.dot(a, b, preferred_element_type=F32)


def dot_nt(a, b):
    return lax.dot_general(a, b, NT, preferred_element_type=F32)


def any_spec():
    return pl.BlockSpec(memory_space=pl.ANY)


def vmem_spec():
    return pl.BlockSpec(memory_space=pltpu.VMEM)


def smem_spec():
    return pl.BlockSpec(memory_space=pltpu.SMEM)


def params():
    return pltpu.CompilerParams(vmem_limit_bytes=VMEM_LIMIT)


def cost(flops, moved):
    return pl.CostEstimate(flops=int(flops * SHARE), bytes_accessed=int(moved * SHARE), transcendentals=0)


def leader(level, group):
    if level == 0:
        return group
    return leader(level - 1, 2 * group + (1 if group % 2 == 0 else 0))


def tree(nodes):
    depth = nodes.bit_length() - 1
    ups = []
    for level in range(1, depth):
        pairs = []
        for group in range(nodes >> level):
            left, right = leader(level - 1, 2 * group), leader(level - 1, 2 * group + 1)
            pairs.append((left, right) if group % 2 == 0 else (right, left))
        ups.append(pairs)
    left, right = leader(depth - 1, 0), leader(depth - 1, 1)
    return ups, [(left, right), (right, left)]


def pick_kernel(nodes, firsts, widths, me_ref, rows_ref, loads_ref, *rest):
    count = len(widths)
    outs, (picked, held, sem, sems) = rest[-count * nodes - 4 : -4], rest[-4:]
    load = pltpu.make_async_copy(loads_ref.at[:, pl.ds(firsts[0], sum(widths))], picked, sem)
    load.start()
    total = loads_ref.shape[0]
    block = total // nodes
    me = me_ref[0]
    tile = 128
    load.wait()
    x = picked[...]
    for k in range(total // tile):
        row = rows_ref[k : k + 1, :]
        column = jnp.broadcast_to(row, (tile, tile)).T
        parts = []
        for j in range(total // tile):
            wanted = lax.broadcasted_iota(jnp.int32, (tile, tile), 1) + j * tile
            parts.append(jnp.where(column == wanted, 1.0, 0.0).astype(BF))
        onehot = jnp.concatenate(parts, axis=1)
        held[k * tile : (k + 1) * tile, :] = dot(onehot, x).astype(BF)
    copies = []
    for c in range(count):
        for s in range(nodes):
            start = pl.multiple_of((me ^ s) * block, block)
            source = held.at[pl.ds(start, block), pl.ds(firsts[c] - firsts[0], widths[c])]
            copies.append(pltpu.make_async_copy(source, outs[c * nodes + s], sems.at[c * nodes + s]))
            copies[-1].start()
    for copy in copies:
        copy.wait()


def pick(nodes, firsts, widths, me, rows, loads, after):
    total = loads.shape[0]
    block = total // nodes
    width, count = sum(widths), len(widths) * nodes
    return pl.pallas_call(
        functools.partial(pick_kernel, nodes, firsts, widths),
        in_specs=[smem_spec(), vmem_spec(), any_spec()] + [any_spec()] * len(after),
        out_specs=[any_spec()] * count,
        out_shape=[jax.ShapeDtypeStruct((block, size), BF) for size in widths for _ in range(nodes)],
        scratch_shapes=[pltpu.VMEM((total, width), BF)] * 2
        + [pltpu.SemaphoreType.DMA, pltpu.SemaphoreType.DMA((count,))],
        compiler_params=params(),
        cost_estimate=cost(2 * total * total * width, 4 * total * width),
        name="pick",
    )(me, rows, loads, *after)


def identity(size):
    same = lax.broadcasted_iota(jnp.int32, (size, size), 0) == lax.broadcasted_iota(jnp.int32, (size, size), 1)
    return jnp.where(same, 1.0, 0.0).astype(BF)


def prep_kernel(rows_ref, couple_ref, inv_ref, *rest):
    outs, scratch, sems = rest[-7:-4], rest[-4:-1], rest[-1]
    spread_ref, spread_t_ref, inv_t_ref = scratch
    leaves, picked, order = couple_ref.shape
    root = spread_ref.shape[0]
    copies = []
    for n in range(leaves):
        c = couple_ref[n]
        at = slice(n * order, (n + 1) * order)
        rows = rows_ref[n : n + 1, :]
        onehot = lax.broadcasted_iota(jnp.int32, (root, picked), 0) == jnp.broadcast_to(rows, (root, picked))
        onehot = jnp.where(onehot, 1.0, 0.0).astype(BF)
        spread_ref[:, at] = dot(onehot, c).astype(BF)
        spread_t_ref[at, :] = dot_nt(c.T, onehot).astype(BF)
        inv_t_ref[n] = inv_ref[n].T
        places = [(slice(None), pl.ds(n * order, order)), (pl.ds(n * order, order),), (n,)]
        for k, place in enumerate(places):
            copies.append(pltpu.make_async_copy(scratch[k].at[place], outs[k].at[place], sems.at[k, n]))
            copies[-1].start()
    for copy in copies:
        copy.wait()


def prep(rows, couple, inv, root, after):
    leaves, picked, order = couple.shape
    shapes = [(root, leaves * order), (leaves * order, root), (leaves, order, order)]
    return pl.pallas_call(
        prep_kernel,
        in_specs=[vmem_spec()] * 3 + [any_spec()] * len(after),
        out_specs=[any_spec()] * 3,
        out_shape=[jax.ShapeDtypeStruct(shape, BF) for shape in shapes],
        scratch_shapes=[pltpu.VMEM(shape, BF) for shape in shapes] + [pltpu.SemaphoreType.DMA((3, leaves))],
        compiler_params=params(),
        cost_estimate=cost(2 * leaves * picked * order * (2 * root + 2 * order), leaves * order * (4 * root + 6 * order)),
        name="prep",
    )(rows, couple, inv, *after)


def forward_kernel(nodes, chunks, me_ref, inv_ref, spread_ref, *rest):
    blocks, (out_ref, *outs), (held, fwd_ref, sem) = rest[:nodes], rest[nodes:-3], rest[-3:]
    block = blocks[0].shape[0]
    leaves, order, _ = inv_ref.shape
    half = order // 2
    me = me_ref[0]
    for s in range(nodes):
        held[pl.ds(pl.multiple_of((me ^ s) * block, block), block), :] = blocks[s][...]
    for n in range(leaves):
        at = n * order
        x = held[at : at + order, :]
        fwd_ref[at : at + half, :] = dot(inv_ref[n, :half, :half], x[:half]).astype(BF)
        fwd_ref[at + half : at + order, :] = dot(inv_ref[n, half:, :], x).astype(BF)
    copy = pltpu.make_async_copy(fwd_ref, out_ref, sem)
    copy.start()
    root = spread_ref.shape[0]
    tile = min(256, root)
    for t in range(root // tile):
        at = slice(t * tile, (t + 1) * tile)
        part = dot(spread_ref[at, :], fwd_ref[...])
        for c in range(chunks):
            piece = part[:, c * LANES : (c + 1) * LANES]
            outs[c][at, :] = piece.astype(BF)
            outs[chunks + c][at, :] = piece
    copy.wait()


def forward(nodes, me, inv, spread, blocks):
    leaves, order, _ = inv.shape
    root = spread.shape[0]
    width = blocks[0].shape[1]
    chunks = width // LANES
    return pl.pallas_call(
        functools.partial(forward_kernel, nodes, chunks),
        in_specs=[smem_spec()] + [vmem_spec()] * (2 + nodes),
        out_specs=[any_spec()] + [vmem_spec()] * (2 * chunks),
        out_shape=[jax.ShapeDtypeStruct((leaves * order, width), BF)]
        + [jax.ShapeDtypeStruct((root, LANES), BF)] * chunks
        + [jax.ShapeDtypeStruct((root, LANES), F32)] * chunks,
        scratch_shapes=[pltpu.VMEM((leaves * order, width), BF)] * 2 + [pltpu.SemaphoreType.DMA],
        compiler_params=params(),
        cost_estimate=cost(
            40 * leaves * order * width * (order + root),
            40 * leaves * order * (order + root + 3 * width) + 6 * root * width,
        ),
        name="forward",
    )(me, inv, spread, *blocks)


def piece_kernel(width, mine_ref, inv_ref, *rest):
    out_ref, sem = rest[-2:]
    start = pl.multiple_of(mine_ref[0] * width, width)
    copy = pltpu.make_async_copy(inv_ref.at[:, pl.ds(start, width)], out_ref, sem)
    copy.start()
    copy.wait()


def take_piece(mine, root_inv, count, after):
    rows, root = root_inv.shape
    width = root // count
    return pl.pallas_call(
        functools.partial(piece_kernel, width),
        in_specs=[smem_spec()] + [any_spec()] * (1 + len(after)),
        out_specs=any_spec(),
        out_shape=jax.ShapeDtypeStruct((rows, width), BF),
        scratch_shapes=[pltpu.SemaphoreType.DMA],
        compiler_params=params(),
        cost_estimate=cost(0, 4 * rows * width),
        name="piece",
    )(mine, root_inv, *after)


def gather_kernel(nodes, me_ref, *rest):
    pieces, (out_ref, sems) = rest[:nodes], rest[-2:]
    rows = pieces[0].shape[0]
    copies = []
    for s in range(nodes):
        at = pl.ds(pl.multiple_of((me_ref[0] ^ s) * rows, rows), rows)
        copies.append(pltpu.make_async_copy(pieces[s], out_ref.at[at], sems.at[s]))
        copies[-1].start()
    for copy in copies:
        copy.wait()


def gather_rows(nodes, me, pieces, after):
    rows, width = pieces[0].shape
    return pl.pallas_call(
        functools.partial(gather_kernel, nodes),
        in_specs=[smem_spec()] + [any_spec()] * (nodes + len(after)),
        out_specs=any_spec(),
        out_shape=jax.ShapeDtypeStruct((nodes * rows, width), BF),
        scratch_shapes=[pltpu.SemaphoreType.DMA((nodes,))],
        compiler_params=params(),
        cost_estimate=cost(0, 4 * nodes * rows * width),
        name="gather_rows",
    )(me, *pieces, *after)


def root_prep_kernel(places, count, mine_ref, pieces_ref, *rest):
    whole_ref, whole_t_ref = rest[-2:]
    root = whole_ref.shape[0]
    width, rows = root // count, root // len(places)
    for q in range(count):
        at = pl.ds(pl.multiple_of((mine_ref[0] ^ q) * width, width), width)
        for k, place in enumerate(places):
            start = q * root + k * rows
            whole_ref[place * rows : (place + 1) * rows, at] = pieces_ref[start : start + rows, :]
    for t in range(count):
        whole_t_ref[t * width : (t + 1) * width, :] = whole_ref[:, t * width : (t + 1) * width].T


def root_prep(mine, places, count, pieces, after):
    root = pieces.shape[1] * count
    return pl.pallas_call(
        functools.partial(root_prep_kernel, places, count),
        in_specs=[smem_spec(), vmem_spec()] + [any_spec()] * len(after),
        out_specs=[vmem_spec()] * 2,
        out_shape=[jax.ShapeDtypeStruct((root, root), BF)] * 2,
        compiler_params=params(),
        cost_estimate=cost(root * root, 6 * root * root),
        name="root_prep",
    )(mine, pieces, *after)


def root_kernel(first, whole_ref, whole_t_ref, loads_ref, one_ref, two_ref, *rest):
    out_ref, reduced, solved = rest[-3:]
    root = whole_ref.shape[0]
    tile = min(256, root)
    update = one_ref[...].astype(F32) + two_ref[...].astype(F32)
    reduced[...] = (loads_ref[:, first : first + out_ref.shape[1]].astype(F32) - update).astype(BF)
    for t in range(root // tile):
        at = slice(t * tile, (t + 1) * tile)
        solved[at, :] = dot(whole_ref[at, : (t + 1) * tile], reduced[: (t + 1) * tile, :]).astype(BF)
    for t in range(root // tile):
        at = slice(t * tile, (t + 1) * tile)
        out_ref[at, :] = dot(whole_t_ref[at, t * tile :], solved[t * tile :, :]).astype(BF)


def root_solve(first, whole, whole_t, root_loads, one, two, after):
    root, width = one.shape
    return pl.pallas_call(
        functools.partial(root_kernel, first),
        in_specs=[vmem_spec()] * 5 + [any_spec()] * len(after),
        out_specs=vmem_spec(),
        out_shape=jax.ShapeDtypeStruct((root, width), BF),
        scratch_shapes=[pltpu.VMEM((root, width), BF)] * 2,
        compiler_params=params(),
        cost_estimate=cost(60 * root * root * width, 60 * root * root + 120 * root * width),
        name="root_solve",
    )(whole, whole_t, root_loads, one, two, *after)


def backward_kernel(first, count, take_ref, fwd_ref, spread_t_ref, inv_t_ref, *rest):
    owns, gots = rest[:count], rest[count : 2 * count]
    out_ref, root_ref, held, solved, sems = rest[-5:]
    leaves, order, _ = inv_t_ref.shape
    half = order // 2
    columns = pl.ds(first, held.shape[1])
    for c in range(count):
        held[:, c * LANES : (c + 1) * LANES] = jnp.where(take_ref[0] > 0, gots[c][...], owns[c][...])
    copies = [pltpu.make_async_copy(held, root_ref.at[:, columns], sems.at[leaves])]
    copies[0].start()
    root_solution = held[...]
    for n in range(leaves):
        at = n * order
        parts = []
        for start in (at, at + half):
            back = dot(spread_t_ref[start : start + half, :], root_solution)
            parts.append((fwd_ref[start : start + half, :].astype(F32) - back).astype(BF))
        x = jnp.concatenate(parts, axis=0)
        solved[at : at + half, :] = dot(inv_t_ref[n, :half, :], x).astype(BF)
        solved[at + half : at + order, :] = dot(inv_t_ref[n, half:, half:], x[half:]).astype(BF)
        rows = pl.ds(at, order)
        copy = pltpu.make_async_copy(solved.at[rows], out_ref.at[rows, columns], sems.at[n])
        copy.start()
        copies.append(copy)
    for copy in copies:
        copy.wait()


def backward(first, total, take, owns, gots, fwd, spread_t, inv_t, before):
    leaves, order, _ = inv_t.shape
    count = len(owns)
    root, width = spread_t.shape[1], count * LANES
    inputs = [take, fwd, spread_t, inv_t, *owns, *gots]
    aliases, extra = {}, []
    if before is not None:
        aliases = {len(inputs): 0, len(inputs) + 1: 1}
        extra = list(before)
    return pl.pallas_call(
        functools.partial(backward_kernel, first, count),
        in_specs=[smem_spec()] + [vmem_spec()] * (len(inputs) - 1) + [any_spec()] * len(extra),
        out_specs=[any_spec()] * 2,
        out_shape=[
            jax.ShapeDtypeStruct((leaves * order, total), BF),
            jax.ShapeDtypeStruct((root, total), BF),
        ],
        scratch_shapes=[
            pltpu.VMEM((root, width), BF),
            pltpu.VMEM((leaves * order, width), BF),
            pltpu.SemaphoreType.DMA((leaves + 1,)),
        ],
        input_output_aliases=aliases,
        compiler_params=params(),
        cost_estimate=cost(
            20 * leaves * order * width * (order + root),
            2 * leaves * order * (order + root + 2 * width) + 6 * root * width,
        ),
        name="backward",
    )(*inputs, *extra)


def per_device(sizes, loads, root_loads, send_rows, leaf_inv, couple, couple_rows, root_inv):
    nodes = sizes["node"]
    root, width = root_loads.shape
    total = loads.shape[0]
    ups, top = tree(nodes)
    node = lax.axis_index("node")
    me = node.astype(jnp.int32).reshape(1)
    rows = send_rows.reshape(total // 128, 128)

    stages, count = [], 1
    for axis in ("rhs", "shift"):
        if count * sizes[axis] * LANES <= root:
            bits = sizes[axis].bit_length() - 1
            stages = [(axis, bit) for bit in reversed(range(bits))] + stages
            count *= sizes[axis]
    mine = jnp.int32(0)
    for place, (axis, bit) in enumerate(stages):
        mine = mine + (((lax.axis_index(axis).astype(jnp.int32) >> bit) & 1) << place)
    mine = mine.reshape(1)
    places = list(range(nodes))

    sizes_of = [min(GROUP * LANES, width - first) for first in range(0, width, GROUP * LANES)]
    firsts = [sum(sizes_of[:g]) for g in range(len(sizes_of))]
    sent = pick(nodes, firsts, sizes_of, me, rows, loads, [])
    piece = take_piece(mine, root_inv, count, [sent[0]])
    pieces = [piece]
    for s in range(1, nodes):
        pieces.append(lax.ppermute(piece, "node", [(i, i ^ s) for i in range(nodes) if i ^ s in top[0]]))
    piece = gather_rows(nodes, me, pieces, [sent[0]])
    for axis, bit in stages:
        pairs = [(i, i ^ (1 << bit)) for i in range(sizes[axis])]
        piece = jnp.concatenate([piece, lax.ppermute(piece, axis, pairs)], axis=0)

    blocks = []
    for g in range(len(sizes_of)):
        own = sent[g * nodes : (g + 1) * nodes]
        pairs = [[(i, i ^ s) for i in range(nodes)] for s in range(nodes)]
        blocks.append([own[0]] + [lax.ppermute(own[s], "node", pairs[s]) for s in range(1, nodes)])
    spread, spread_t, inv_t = prep(couple_rows, couple, leaf_inv, root, [sent[0]])
    whole, whole_t = root_prep(mine, places, count, piece, [])
    result = None
    for g in range(len(sizes_of)):
        fwd, *parts = forward(nodes, me, leaf_inv, spread, blocks[g])
        owns, gots = [], []
        chunks = sizes_of[g] // LANES
        for c in range(chunks):
            part, wide = parts[c], parts[chunks + c]
            for pairs in ups:
                wide = wide + lax.ppermute(part, "node", pairs).astype(F32)
                part = wide.astype(BF)
            other = lax.ppermute(part, "node", top)
            own = root_solve(firsts[g] + c * LANES, whole, whole_t, root_loads, part, other, [])
            got, take = own, jnp.zeros((1,), jnp.int32)
            for level, pairs in enumerate(reversed(ups)):
                if level > 0:
                    own = jnp.where(take[0] > 0, got, own)
                got = lax.ppermute(own, "node", [(b, a) for a, b in pairs])
                take = jnp.zeros((1,), jnp.int32)
                for sender, _ in pairs:
                    take = take + (node == sender).astype(jnp.int32)
            owns.append(own)
            gots.append(got)
        result = backward(firsts[g], width, take, owns, gots, fwd, spread_t, inv_t, result)
    return tuple(result)


def solution(mesh):
    return jax.shard_map(
        functools.partial(per_device, dict(mesh.shape)),
        mesh=mesh,
        in_specs=(
            P("node", ("shift", "rhs")),
            P(None, ("shift", "rhs")),
            P("node"),
            P("node", None, None),
            P("node", None, None),
            P("node", None),
            P("node", None),
        ),
        out_specs=(P("node", ("shift", "rhs")), P(None, ("shift", "rhs"))),
        check_vma=False,
    )
```

```python
import functools

import jax
import jax.numpy as jnp
from jax import lax
from jax.experimental import pallas as pl
from jax.experimental.pallas import tpu as pltpu
from jax.sharding import PartitionSpec as P

BF = jnp.bfloat16
F32 = jnp.float32
LANES = 128
GROUP = 2
SHARE = 1.0
VMEM_LIMIT = 24 * 1024 * 1024
NT = (((1,), (1,)), ((), ()))


def dot(a, b):
    return jnp.dot(a, b, preferred_element_type=F32)


def dot_nt(a, b):
    return lax.dot_general(a, b, NT, preferred_element_type=F32)


def any_spec():
    return pl.BlockSpec(memory_space=pl.ANY)


def vmem_spec():
    return pl.BlockSpec(memory_space=pltpu.VMEM)


def smem_spec():
    return pl.BlockSpec(memory_space=pltpu.SMEM)


def params():
    return pltpu.CompilerParams(vmem_limit_bytes=VMEM_LIMIT)


def cost(flops, moved):
    return pl.CostEstimate(flops=int(flops * SHARE), bytes_accessed=int(moved * SHARE), transcendentals=0)


def leader(level, group):
    if level == 0:
        return group
    return leader(level - 1, 2 * group + (1 if group % 2 == 0 else 0))


def tree(nodes):
    depth = nodes.bit_length() - 1
    ups = []
    for level in range(1, depth):
        pairs = []
        for group in range(nodes >> level):
            left, right = leader(level - 1, 2 * group), leader(level - 1, 2 * group + 1)
            pairs.append((left, right) if group % 2 == 0 else (right, left))
        ups.append(pairs)
    left, right = leader(depth - 1, 0), leader(depth - 1, 1)
    return ups, [(left, right), (right, left)]


def pick_kernel(nodes, firsts, widths, me_ref, rows_ref, loads_ref, *rest):
    count = len(widths)
    outs, (picked, held, sem, sems) = rest[-count * nodes - 4 : -4], rest[-4:]
    load = pltpu.make_async_copy(loads_ref.at[:, pl.ds(firsts[0], sum(widths))], picked, sem)
    load.start()
    total = loads_ref.shape[0]
    block = total // nodes
    me = me_ref[0]
    tile = 128
    load.wait()
    x = picked[...]
    for k in range(total // tile):
        row = rows_ref[k : k + 1, :]
        column = jnp.broadcast_to(row, (tile, tile)).T
        parts = []
        for j in range(total // tile):
            wanted = lax.broadcasted_iota(jnp.int32, (tile, tile), 1) + j * tile
            parts.append(jnp.where(column == wanted, 1.0, 0.0).astype(BF))
        onehot = jnp.concatenate(parts, axis=1)
        held[k * tile : (k + 1) * tile, :] = dot(onehot, x).astype(BF)
    copies = []
    for c in range(count):
        for s in range(nodes):
            start = pl.multiple_of((me ^ s) * block, block)
            source = held.at[pl.ds(start, block), pl.ds(firsts[c] - firsts[0], widths[c])]
            copies.append(pltpu.make_async_copy(source, outs[c * nodes + s], sems.at[c * nodes + s]))
            copies[-1].start()
    for copy in copies:
        copy.wait()


def pick(nodes, firsts, widths, me, rows, loads, after):
    total = loads.shape[0]
    block = total // nodes
    width, count = sum(widths), len(widths) * nodes
    return pl.pallas_call(
        functools.partial(pick_kernel, nodes, firsts, widths),
        in_specs=[smem_spec(), vmem_spec(), any_spec()] + [any_spec()] * len(after),
        out_specs=[any_spec()] * count,
        out_shape=[jax.ShapeDtypeStruct((block, size), BF) for size in widths for _ in range(nodes)],
        scratch_shapes=[pltpu.VMEM((total, width), BF)] * 2
        + [pltpu.SemaphoreType.DMA, pltpu.SemaphoreType.DMA((count,))],
        compiler_params=params(),
        cost_estimate=cost(2 * total * total * width, 4 * total * width),
        name="pick",
    )(me, rows, loads, *after)


def identity(size):
    same = lax.broadcasted_iota(jnp.int32, (size, size), 0) == lax.broadcasted_iota(jnp.int32, (size, size), 1)
    return jnp.where(same, 1.0, 0.0).astype(BF)


def prep_kernel(rows_ref, couple_ref, inv_ref, *rest):
    outs, scratch, sems = rest[-7:-4], rest[-4:-1], rest[-1]
    spread_ref, spread_t_ref, inv_t_ref = scratch
    leaves, picked, order = couple_ref.shape
    root = spread_ref.shape[0]
    copies = []
    for n in range(leaves):
        c = couple_ref[n]
        at = slice(n * order, (n + 1) * order)
        rows = rows_ref[n : n + 1, :]
        onehot = lax.broadcasted_iota(jnp.int32, (root, picked), 0) == jnp.broadcast_to(rows, (root, picked))
        onehot = jnp.where(onehot, 1.0, 0.0).astype(BF)
        spread_ref[:, at] = dot(onehot, c).astype(BF)
        spread_t_ref[at, :] = dot_nt(c.T, onehot).astype(BF)
        inv_t_ref[n] = inv_ref[n].T
        places = [(slice(None), pl.ds(n * order, order)), (pl.ds(n * order, order),), (n,)]
        for k, place in enumerate(places):
            copies.append(pltpu.make_async_copy(scratch[k].at[place], outs[k].at[place], sems.at[k, n]))
            copies[-1].start()
    for copy in copies:
        copy.wait()


def prep(rows, couple, inv, root, after):
    leaves, picked, order = couple.shape
    shapes = [(root, leaves * order), (leaves * order, root), (leaves, order, order)]
    return pl.pallas_call(
        prep_kernel,
        in_specs=[vmem_spec()] * 3 + [any_spec()] * len(after),
        out_specs=[any_spec()] * 3,
        out_shape=[jax.ShapeDtypeStruct(shape, BF) for shape in shapes],
        scratch_shapes=[pltpu.VMEM(shape, BF) for shape in shapes] + [pltpu.SemaphoreType.DMA((3, leaves))],
        compiler_params=params(),
        cost_estimate=cost(2 * leaves * picked * order * (2 * root + 2 * order), leaves * order * (4 * root + 6 * order)),
        name="prep",
    )(rows, couple, inv, *after)


def forward_kernel(nodes, chunks, me_ref, inv_ref, spread_ref, *rest):
    blocks, (out_ref, *outs), (held, fwd_ref, sem) = rest[:nodes], rest[nodes:-3], rest[-3:]
    block = blocks[0].shape[0]
    leaves, order, _ = inv_ref.shape
    half = order // 2
    me = me_ref[0]
    for s in range(nodes):
        held[pl.ds(pl.multiple_of((me ^ s) * block, block), block), :] = blocks[s][...]
    for n in range(leaves):
        at = n * order
        x = held[at : at + order, :]
        fwd_ref[at : at + half, :] = dot(inv_ref[n, :half, :half], x[:half]).astype(BF)
        fwd_ref[at + half : at + order, :] = dot(inv_ref[n, half:, :], x).astype(BF)
    copy = pltpu.make_async_copy(fwd_ref, out_ref, sem)
    copy.start()
    root = spread_ref.shape[0]
    tile = min(256, root)
    for t in range(root // tile):
        at = slice(t * tile, (t + 1) * tile)
        part = dot(spread_ref[at, :], fwd_ref[...])
        for c in range(chunks):
            piece = part[:, c * LANES : (c + 1) * LANES]
            outs[c][at, :] = piece.astype(BF)
            outs[chunks + c][at, :] = piece
    copy.wait()


def forward(nodes, me, inv, spread, blocks):
    leaves, order, _ = inv.shape
    root = spread.shape[0]
    width = blocks[0].shape[1]
    chunks = width // LANES
    return pl.pallas_call(
        functools.partial(forward_kernel, nodes, chunks),
        in_specs=[smem_spec()] + [vmem_spec()] * (2 + nodes),
        out_specs=[any_spec()] + [vmem_spec()] * (2 * chunks),
        out_shape=[jax.ShapeDtypeStruct((leaves * order, width), BF)]
        + [jax.ShapeDtypeStruct((root, LANES), BF)] * chunks
        + [jax.ShapeDtypeStruct((root, LANES), F32)] * chunks,
        scratch_shapes=[pltpu.VMEM((leaves * order, width), BF)] * 2 + [pltpu.SemaphoreType.DMA],
        compiler_params=params(),
        cost_estimate=cost(
            40 * leaves * order * width * (order + root),
            40 * leaves * order * (order + root + 3 * width) + 6 * root * width,
        ),
        name="forward",
    )(me, inv, spread, *blocks)


def piece_kernel(width, mine_ref, inv_ref, *rest):
    out_ref, sem = rest[-2:]
    start = pl.multiple_of(mine_ref[0] * width, width)
    copy = pltpu.make_async_copy(inv_ref.at[:, pl.ds(start, width)], out_ref, sem)
    copy.start()
    copy.wait()


def take_piece(mine, root_inv, count, after):
    rows, root = root_inv.shape
    width = root // count
    return pl.pallas_call(
        functools.partial(piece_kernel, width),
        in_specs=[smem_spec()] + [any_spec()] * (1 + len(after)),
        out_specs=any_spec(),
        out_shape=jax.ShapeDtypeStruct((rows, width), BF),
        scratch_shapes=[pltpu.SemaphoreType.DMA],
        compiler_params=params(),
        cost_estimate=cost(0, 4 * rows * width),
        name="piece",
    )(mine, root_inv, *after)


def gather_kernel(nodes, me_ref, *rest):
    pieces, (out_ref, sems) = rest[:nodes], rest[-2:]
    rows = pieces[0].shape[0]
    copies = []
    for s in range(nodes):
        at = pl.ds(pl.multiple_of((me_ref[0] ^ s) * rows, rows), rows)
        copies.append(pltpu.make_async_copy(pieces[s], out_ref.at[at], sems.at[s]))
        copies[-1].start()
    for copy in copies:
        copy.wait()


def gather_rows(nodes, me, pieces, after):
    rows, width = pieces[0].shape
    return pl.pallas_call(
        functools.partial(gather_kernel, nodes),
        in_specs=[smem_spec()] + [any_spec()] * (nodes + len(after)),
        out_specs=any_spec(),
        out_shape=jax.ShapeDtypeStruct((nodes * rows, width), BF),
        scratch_shapes=[pltpu.SemaphoreType.DMA((nodes,))],
        compiler_params=params(),
        cost_estimate=cost(0, 4 * nodes * rows * width),
        name="gather_rows",
    )(me, *pieces, *after)


def root_prep_kernel(places, count, mine_ref, pieces_ref, *rest):
    whole_ref, whole_t_ref = rest[-2:]
    root = whole_ref.shape[0]
    width, rows = root // count, root // len(places)
    for q in range(count):
        at = pl.ds(pl.multiple_of((mine_ref[0] ^ q) * width, width), width)
        for k, place in enumerate(places):
            start = q * root + k * rows
            whole_ref[place * rows : (place + 1) * rows, at] = pieces_ref[start : start + rows, :]
    for t in range(count):
        whole_t_ref[t * width : (t + 1) * width, :] = whole_ref[:, t * width : (t + 1) * width].T


def root_prep(mine, places, count, pieces, after):
    root = pieces.shape[1] * count
    return pl.pallas_call(
        functools.partial(root_prep_kernel, places, count),
        in_specs=[smem_spec(), vmem_spec()] + [any_spec()] * len(after),
        out_specs=[vmem_spec()] * 2,
        out_shape=[jax.ShapeDtypeStruct((root, root), BF)] * 2,
        compiler_params=params(),
        cost_estimate=cost(root * root, 6 * root * root),
        name="root_prep",
    )(mine, pieces, *after)


def root_kernel(first, whole_ref, whole_t_ref, loads_ref, one_ref, two_ref, *rest):
    out_ref, reduced, solved = rest[-3:]
    root = whole_ref.shape[0]
    tile = min(256, root)
    update = one_ref[...].astype(F32) + two_ref[...].astype(F32)
    reduced[...] = (loads_ref[:, first : first + out_ref.shape[1]].astype(F32) - update).astype(BF)
    for t in range(root // tile):
        at = slice(t * tile, (t + 1) * tile)
        solved[at, :] = dot(whole_ref[at, : (t + 1) * tile], reduced[: (t + 1) * tile, :]).astype(BF)
    for t in range(root // tile):
        at = slice(t * tile, (t + 1) * tile)
        out_ref[at, :] = dot(whole_t_ref[at, t * tile :], solved[t * tile :, :]).astype(BF)


def root_solve(first, whole, whole_t, root_loads, one, two, after):
    root, width = one.shape
    return pl.pallas_call(
        functools.partial(root_kernel, first),
        in_specs=[vmem_spec()] * 5 + [any_spec()] * len(after),
        out_specs=vmem_spec(),
        out_shape=jax.ShapeDtypeStruct((root, width), BF),
        scratch_shapes=[pltpu.VMEM((root, width), BF)] * 2,
        compiler_params=params(),
        cost_estimate=cost(60 * root * root * width, 60 * root * root + 120 * root * width),
        name="root_solve",
    )(whole, whole_t, root_loads, one, two, *after)


def backward_kernel(first, count, take_ref, fwd_ref, spread_t_ref, inv_t_ref, *rest):
    owns, gots = rest[:count], rest[count : 2 * count]
    out_ref, root_ref, held, solved, sems = rest[-5:]
    leaves, order, _ = inv_t_ref.shape
    half = order // 2
    columns = pl.ds(first, held.shape[1])
    for c in range(count):
        held[:, c * LANES : (c + 1) * LANES] = jnp.where(take_ref[0] > 0, gots[c][...], owns[c][...])
    copies = [pltpu.make_async_copy(held, root_ref.at[:, columns], sems.at[leaves])]
    copies[0].start()
    root_solution = held[...]
    for n in range(leaves):
        at = n * order
        parts = []
        for start in (at, at + half):
            back = dot(spread_t_ref[start : start + half, :], root_solution)
            parts.append((fwd_ref[start : start + half, :].astype(F32) - back).astype(BF))
        x = jnp.concatenate(parts, axis=0)
        solved[at : at + half, :] = dot(inv_t_ref[n, :half, :], x).astype(BF)
        solved[at + half : at + order, :] = dot(inv_t_ref[n, half:, half:], x[half:]).astype(BF)
        rows = pl.ds(at, order)
        copy = pltpu.make_async_copy(solved.at[rows], out_ref.at[rows, columns], sems.at[n])
        copy.start()
        copies.append(copy)
    for copy in copies:
        copy.wait()


def backward(first, total, take, owns, gots, fwd, spread_t, inv_t, before):
    leaves, order, _ = inv_t.shape
    count = len(owns)
    root, width = spread_t.shape[1], count * LANES
    inputs = [take, fwd, spread_t, inv_t, *owns, *gots]
    aliases, extra = {}, []
    if before is not None:
        aliases = {len(inputs): 0, len(inputs) + 1: 1}
        extra = list(before)
    return pl.pallas_call(
        functools.partial(backward_kernel, first, count),
        in_specs=[smem_spec()] + [vmem_spec()] * (len(inputs) - 1) + [any_spec()] * len(extra),
        out_specs=[any_spec()] * 2,
        out_shape=[
            jax.ShapeDtypeStruct((leaves * order, total), BF),
            jax.ShapeDtypeStruct((root, total), BF),
        ],
        scratch_shapes=[
            pltpu.VMEM((root, width), BF),
            pltpu.VMEM((leaves * order, width), BF),
            pltpu.SemaphoreType.DMA((leaves + 1,)),
        ],
        input_output_aliases=aliases,
        compiler_params=params(),
        cost_estimate=cost(
            20 * leaves * order * width * (order + root),
            2 * leaves * order * (order + root + 2 * width) + 6 * root * width,
        ),
        name="backward",
    )(*inputs, *extra)


def per_device(sizes, loads, root_loads, send_rows, leaf_inv, couple, couple_rows, root_inv):
    nodes = sizes["node"]
    root, width = root_loads.shape
    total = loads.shape[0]
    ups, top = tree(nodes)
    node = lax.axis_index("node")
    me = node.astype(jnp.int32).reshape(1)
    rows = send_rows.reshape(total // 128, 128)

    stages, count = [], 1
    for axis in ("rhs", "shift"):
        if count * sizes[axis] * LANES <= root:
            bits = sizes[axis].bit_length() - 1
            stages = [(axis, bit) for bit in reversed(range(bits))] + stages
            count *= sizes[axis]
    mine = jnp.int32(0)
    for place, (axis, bit) in enumerate(stages):
        mine = mine + (((lax.axis_index(axis).astype(jnp.int32) >> bit) & 1) << place)
    mine = mine.reshape(1)
    places = list(range(nodes))

    sizes_of = [min(GROUP * LANES, width - first) for first in range(0, width, GROUP * LANES)]
    firsts = [sum(sizes_of[:g]) for g in range(len(sizes_of))]
    sent = pick(nodes, firsts, sizes_of, me, rows, loads, [])
    piece = take_piece(mine, root_inv, count, [])
    pieces = [piece]
    for s in range(1, nodes):
        pieces.append(lax.ppermute(piece, "node", [(i, i ^ s) for i in range(nodes) if i ^ s in top[0]]))
    piece = gather_rows(nodes, me, pieces, [sent[0]])
    for axis, bit in stages:
        pairs = [(i, i ^ (1 << bit)) for i in range(sizes[axis])]
        piece = jnp.concatenate([piece, lax.ppermute(piece, axis, pairs)], axis=0)

    blocks = []
    for g in range(len(sizes_of)):
        own = sent[g * nodes : (g + 1) * nodes]
        pairs = [[(i, i ^ s) for i in range(nodes)] for s in range(nodes)]
        blocks.append([own[0]] + [lax.ppermute(own[s], "node", pairs[s]) for s in range(1, nodes)])
    spread, spread_t, inv_t = prep(couple_rows, couple, leaf_inv, root, [sent[0]])
    whole, whole_t = root_prep(mine, places, count, piece, [])
    result = None
    for g in range(len(sizes_of)):
        fwd, *parts = forward(nodes, me, leaf_inv, spread, blocks[g])
        owns, gots = [], []
        chunks = sizes_of[g] // LANES
        for c in range(chunks):
            part, wide = parts[c], parts[chunks + c]
            for pairs in ups:
                wide = wide + lax.ppermute(part, "node", pairs).astype(F32)
                part = wide.astype(BF)
            other = lax.ppermute(part, "node", top)
            own = root_solve(firsts[g] + c * LANES, whole, whole_t, root_loads, part, other, [])
            got, take = own, jnp.zeros((1,), jnp.int32)
            for level, pairs in enumerate(reversed(ups)):
                if level > 0:
                    own = jnp.where(take[0] > 0, got, own)
                got = lax.ppermute(own, "node", [(b, a) for a, b in pairs])
                take = jnp.zeros((1,), jnp.int32)
                for sender, _ in pairs:
                    take = take + (node == sender).astype(jnp.int32)
            owns.append(own)
            gots.append(got)
        result = backward(firsts[g], width, take, owns, gots, fwd, spread_t, inv_t, result)
    return tuple(result)


def solution(mesh):
    return jax.shard_map(
        functools.partial(per_device, dict(mesh.shape)),
        mesh=mesh,
        in_specs=(
            P("node", ("shift", "rhs")),
            P(None, ("shift", "rhs")),
            P("node"),
            P("node", None, None),
            P("node", None, None),
            P("node", None),
            P("node", None),
        ),
        out_specs=(P("node", ("shift", "rhs")), P(None, ("shift", "rhs"))),
        check_vma=False,
    )
```
